32 devices in a mesh: grp: 2 (over y), sec: 4 (over z), term: 4 (over x, core).
Axes of the slice: x: 2, y: 2, z: 4, core: 2. Of those that a mesh axis runs over, the one named last changes fastest.
Arguments:
- wavefunction: bfloat16 [16, 16, 2, 128, 128], P(('grp', 'sec')), parts along dimension 0, may hold values from -6 to 6
- left_window: bfloat16 [16, 48, 32, 128], P(('grp', 'sec'), 'term'), parts along dimension 0, may hold values from -0.5 to 0.5
- right_blocks: bfloat16 [16, 48, 128, 128], P(('grp', 'sec'), 'term'), parts along dimension 0, may hold values from -0.5 to 0.5
- couplings: float32 [48, 16], P('term'), may hold values from -0.875 to 0.875
- sector_order: int32 [16], P('grp'), parts along dimension 0, may hold values from 64 to 128
- partner: int32 [16, 16], P('grp'), parts along dimension 0, may hold values from 0 to 7, as said below
Outputs:
- products_out: bfloat16 [16, 16, 2, 32, 128], P(('grp', 'sec'), None, None, 'term'), parts along dimension 0
The draws below stay inside these ranges and needn't reach their ends.
There are 2 independent parts, one for each index of `grp`. The reference program is written for one: setup_inputs(seed, part) draws one part's arguments, and reference() takes and returns one part's arrays. A program takes and returns all parts, laid end to end along the dimension named above; an argument that names none is the same for every part. Nothing has to cross between parts.
Inputs may be any that keep to these rules, and one draw needn't show every extreme that they name: The right sector partner[a, s] belongs to index partner[a, s] // 2 of sec. Of the 2 x 16 blocks of the sectors of one index of sec, at most 8 have right sectors of any one index, and that many is reached in every draw.
All inputs are finite; a program needn't handle non-finite values.
Results may differ from the reference program's by a relative error of at most 0.005.
Values may be sent and summed in bfloat16 or wider, within the bound.
No kernel may reach another device: no remote copies, remote signals or barrier semaphores. Data moves between devices by JAX's collectives and lax.ppermute only.
A program may use at most 128 MiB of HBM per device.

```python
import jax
import jax.numpy as jnp
from jax import lax

SECTOR = 128
STATES = 16
ROWS = 32
SEC_DEV = 2
SECTORS = 8
TERMS = 48
CAPACITY = 8
N_SEC = 4


def draw_partner(key, part):
    key = jax.random.fold_in(key, 7)
    block_count = SEC_DEV * STATES
    pool_size = CAPACITY * N_SEC

    def per_source(source_key):
        first_key, second_key = jax.random.split(source_key)
        offsets = jax.random.permutation(first_key, pool_size)[:block_count] % N_SEC
        within = jax.random.randint(second_key, (block_count,), 0, SEC_DEV)
        return (offsets, within)
    offsets, within = jax.vmap(per_source)(jax.random.split(key, N_SEC))
    source = jnp.arange(N_SEC, dtype=jnp.int32)[:, None]
    target = (source + offsets) % N_SEC
    partner_ids = target * SEC_DEV + within
    return partner_ids.reshape(SECTORS, STATES).astype(jnp.int32)


def touch_ends(values, key, smallest, top_value):
    dims = values.shape
    spot = [jax.random.randint(jax.random.fold_in(key, axis), (), 0, dims[axis]) for axis in range(len(dims))]
    values = values.at[tuple(spot)].set(smallest)
    longest = dims.index(max(dims))
    spot[longest] = (spot[longest] + 1) % dims[longest]
    return values.at[tuple(spot)].set(top_value)


def steps_of(stream_key, shape, shards, low, largest):
    factor_of = 1.0
    for dim, parts in shards:
        heights = jax.random.uniform(jax.random.fold_in(jax.random.fold_in(stream_key, 6), dim), (parts,), jnp.float32, low / len(shards), largest / len(shards))
        factor_of = factor_of * jnp.repeat(jnp.exp(heights), shape[dim] // parts).reshape((-1,) + (1,) * (len(shape) - 1 - dim))
    return factor_of


def noise(key, dims, scale, bound, pieces=(), kind=jnp.bfloat16):
    entries = scale * jax.random.normal(key, dims, jnp.float32)
    if pieces:
        entries = entries * steps_of(key, dims, pieces, -0.22, 0.18)
    return jnp.clip(entries, -bound, bound).astype(kind)


def setup_inputs(seed: int = 0, part: int = 0) -> dict:
    key_list = jax.random.split(jax.random.key(seed), 7)
    part_keys = jax.random.split(jax.random.fold_in(key_list[6], part), 7)
    return {
        "wavefunction": noise(part_keys[0], (SECTORS, STATES, 2, SECTOR, SECTOR), 1.0, 6.0, ((0, 4),)),
        "left_window": noise(part_keys[1], (SECTORS, TERMS, ROWS, SECTOR), SECTOR ** -0.5, 0.5, ((0, 4), (1, 4))),
        "right_blocks": noise(part_keys[2], (SECTORS, TERMS, SECTOR, SECTOR), SECTOR ** -0.5, 0.5, ((0, 4), (1, 4))),
        "couplings": noise(key_list[3], (TERMS, STATES), TERMS ** -0.5, 0.875, ((0, 4),), jnp.float32),
        "sector_order": touch_ends(jax.random.randint(part_keys[4], (SECTORS,), SECTOR // 2, SECTOR + 1), jax.random.fold_in(part_keys[4], 1), SECTOR // 2, SECTOR).astype(jnp.int32),
        "partner": draw_partner(jax.random.fold_in(jax.random.fold_in(key_list[6], part), 71), part),
    }


def reference(wavefunction, left_window, right_blocks, couplings, sector_order, partner):
    column_index = jnp.arange(SECTOR, dtype=jnp.int32)

    def sector(which):
        block_data = wavefunction[which]
        left_rows = left_window[which]
        partner_ids = partner[which]
        left_order = sector_order[which]
        right_order = sector_order[partner_ids]
        row_keep = column_index < left_order
        col_keep = column_index[None, :] < right_order[:, None]
        keep_mask = row_keep[None, None, :, None] & col_keep[:, None, None, :]
        masked = block_data * keep_mask.astype(jnp.bfloat16)
        products = jnp.einsum("trn,cvnj->cvtrj", left_rows.astype(jnp.float32), masked.astype(jnp.float32))
        products = (products * jnp.transpose(couplings)[:, None, :, None, None]).astype(jnp.bfloat16)
        picked = right_blocks[partner_ids]
        result = jnp.einsum("cvtrn,ctnk->cvrk", products.astype(jnp.float32), picked.astype(jnp.float32))
        result = result * col_keep.astype(jnp.float32)[:, None, None, :]
        return result.astype(jnp.bfloat16)

    return lax.map(sector, jnp.arange(SECTORS, dtype=jnp.int32))
```

```python
import functools
import math

import jax
import jax.numpy as jnp
from jax import lax
from jax.experimental import pallas as pl
from jax.experimental.pallas import tpu as pltpu
from jax.sharding import PartitionSpec as P

SECTOR = 128
STATES = 16
ROWS = 32
SEC_DEV = 2


def lookup(values_table, indices):
    columns = jnp.arange(values_table.shape[0], dtype=jnp.int32)
    matched = (indices[..., None] == columns).astype(jnp.int32)
    return jnp.sum(matched * values_table, axis=-1)


def general_body(wavefunction, left_window, right_blocks, couplings, sector_order, partner):
    devices = lax.axis_size("sec")
    myself = lax.axis_index("sec")
    block_count = SEC_DEV * STATES
    capacity = max(1, block_count // devices)
    slot_count = devices * capacity
    term_local = left_window.shape[1]
    column_index = jnp.arange(SECTOR, dtype=jnp.int32)
    positions = jnp.arange(block_count, dtype=jnp.int32)
    partner_all = partner.reshape(devices, block_count)
    owner_all = partner_all // SEC_DEV
    earlier = positions[None, :] < positions[:, None]
    same_owner = owner_all[:, :, None] == owner_all[:, None, :]
    rank_all = jnp.sum((same_owner & earlier[None]).astype(jnp.int32), axis=2)
    own_owner = lax.dynamic_index_in_dim(owner_all, myself, 0, keepdims=False)
    own_rank = lax.dynamic_index_in_dim(rank_all, myself, 0, keepdims=False)
    own_partner = lax.dynamic_index_in_dim(partner_all, myself, 0, keepdims=False)
    send_slot = own_owner * capacity + own_rank
    slot_index = jnp.arange(capacity, dtype=jnp.int32)
    matches = (owner_all == myself)[:, :, None] & (
        rank_all[:, :, None] == slot_index[None, None, :]
    )
    hit_int = matches.astype(jnp.int32)
    incoming_partner = jnp.sum(hit_int * partner_all[:, :, None], axis=1).reshape(slot_count)
    incoming_state = jnp.sum(hit_int * (positions % STATES)[None, :, None], axis=1).reshape(
        slot_count
    )
    incoming_local = incoming_partner % SEC_DEV
    incoming_order = lookup(sector_order, incoming_partner)
    column_mask = (column_index[None, :] < incoming_order[:, None]).astype(jnp.float32)
    left_order = lax.dynamic_slice_in_dim(sector_order, myself * SEC_DEV, SEC_DEV)
    right_order = lookup(sector_order, own_partner).reshape(SEC_DEV, STATES)
    row_keep = column_index[None, :] < left_order[:, None]
    col_keep = column_index[None, None, :] < right_order[:, :, None]
    keep_mask = (row_keep[:, None, None, :, None] & col_keep[:, :, None, None, :]).astype(
        jnp.bfloat16
    )
    masked = wavefunction * keep_mask
    groups = math.gcd(slot_count, 8)
    per_group = slot_count // groups

    def right_product(partials, chosen, mask_rows):
        picked = jnp.take(right_blocks, chosen, axis=0)
        result = jnp.einsum(
            "gvtrn,gtnk->gvrk", partials, picked, preferred_element_type=jnp.float32
        )
        return result * mask_rows[:, None, None, :]

    vectors = masked.reshape(block_count, 2, SECTOR, SECTOR)
    left_rows = jnp.take(left_window, positions // STATES, axis=0)
    vector_slots = (
        jnp.zeros((slot_count, 2, SECTOR, SECTOR), jnp.bfloat16).at[send_slot].set(vectors)
    )
    row_slots = (
        jnp.zeros((slot_count, term_local, ROWS, SECTOR), jnp.bfloat16).at[send_slot].set(left_rows)
    )
    vector_in, rows_in = (
        lax.all_to_all(vector_slots, "sec", split_axis=0, concat_axis=0, tiled=True),
        lax.all_to_all(row_slots, "sec", split_axis=0, concat_axis=0, tiled=True),
    )
    slot_coupling = jnp.transpose(jnp.take(couplings, incoming_state, axis=1))

    def grouped_both(inputs):
        vector_group, rows_group, coupling_group, chosen_group, mask_group = inputs
        partials = jnp.einsum(
            "gtrn,gvnj->gvtrj", rows_group, vector_group, preferred_element_type=jnp.float32
        )
        partials = (partials * coupling_group[:, None, :, None, None]).astype(jnp.bfloat16)
        return right_product(partials, chosen_group, mask_group)

    outcome = lax.map(
        grouped_both,
        (
            vector_in.reshape(groups, per_group, 2, SECTOR, SECTOR),
            rows_in.reshape(groups, per_group, term_local, ROWS, SECTOR),
            slot_coupling.reshape(groups, per_group, term_local),
            incoming_local.reshape(groups, per_group),
            column_mask.reshape(groups, per_group, SECTOR),
        ),
    )
    outcome = outcome.reshape(slot_count, 2, ROWS, SECTOR)
    returned_rows = lax.all_to_all(outcome, "sec", split_axis=0, concat_axis=0, tiled=True)
    own_rows = jnp.take(returned_rows, send_slot, axis=0).reshape(SEC_DEV, STATES, 2, ROWS, SECTOR)
    summed = lax.psum_scatter(own_rows, "term", scatter_dimension=3, tiled=True)
    return summed.astype(jnp.bfloat16)


ANY = pl.BlockSpec(memory_space=pl.ANY)
VMEM = pl.BlockSpec(memory_space=pltpu.VMEM)
SMEM = pl.BlockSpec(memory_space=pltpu.SMEM)


def exchange(x, axis, step):
    size = lax.axis_size(axis)
    return lax.ppermute(x, axis, [(i, i ^ step) for i in range(size)])


def gather_pieces(x, axis):
    pieces = [x]
    bit = lax.axis_size(axis) // 2
    while bit:
        pieces = pieces + [exchange(piece, axis, bit) for piece in pieces]
        bit //= 2
    return pieces


def piece_order(size):
    order = [0]
    bit = size // 2
    while bit:
        order = order + [j ^ bit for j in order]
        bit //= 2
    return order


def pack_kernel(devices, terms, partner, wave, left, *refs):
    sends = refs[: devices - 1]
    left_out, counts, table, sems = refs[devices - 1 :]
    capacity = SEC_DEV * STATES // devices
    share = capacity // terms
    me, term = lax.axis_index("sec"), lax.axis_index("term")
    for owner in range(devices):
        counts[owner] = 0

    def place(n, carry):
        owner = partner[me * SEC_DEV + n // STATES, n % STATES] // SEC_DEV
        rank = counts[owner]
        counts[owner] = rank + 1
        table[owner * capacity + rank] = n
        return carry

    lax.fori_loop(0, SEC_DEV * STATES, place, 0)
    copies = []
    for step in range(1, devices):
        target = me ^ step
        for sub in range(share):
            n = table[target * capacity + term * share + sub]
            copy = pltpu.make_async_copy(
                wave.at[n], sends[step - 1].at[sub], sems.at[(step - 1) * share + sub]
            )
            copy.start()
            copies.append(copy)
    local = left.shape[1]
    group = ROWS // terms
    for a in range(SEC_DEV):
        for t in range(0, local, 2):
            first = left[a, t].astype(jnp.float32)
            second = left[a, t + 1].astype(jnp.float32)
            for piece in range(terms):
                rows = slice(piece * group, (piece + 1) * group)
                pair = jnp.concatenate([first[rows], second[rows]], axis=0)
                left_out[piece, a, t * group : (t + 2) * group, :] = pair.astype(jnp.bfloat16)
    for copy in copies:
        copy.wait()


def pack(wave, left, partner, devices, terms):
    capacity = SEC_DEV * STATES // devices
    share = capacity // terms
    local = left.shape[1]
    piece = jax.ShapeDtypeStruct((share, 2, SECTOR, SECTOR), jnp.bfloat16)
    rows = jax.ShapeDtypeStruct((terms, SEC_DEV, local * (ROWS // terms), SECTOR), jnp.bfloat16)
    outs = pl.pallas_call(
        functools.partial(pack_kernel, devices, terms),
        out_shape=[piece] * (devices - 1) + [rows],
        in_specs=[SMEM, ANY, VMEM],
        out_specs=[ANY] * (devices - 1) + [VMEM],
        scratch_shapes=[
            pltpu.SMEM((devices,), jnp.int32),
            pltpu.SMEM((SEC_DEV * STATES,), jnp.int32),
            pltpu.SemaphoreType.DMA(((devices - 1) * share,)),
        ],
        cost_estimate=pl.CostEstimate(flops=0, bytes_accessed=4 << 20, transcendentals=0),
        name="pack",
    )(partner, wave, left)
    return outs[: devices - 1], outs[devices - 1]


def compute_kernel(step, devices, terms, partner, order, coef, *refs):
    pieces = refs[: 1 if step == 0 else terms]
    refs = refs[len(pieces) :]
    left, rights, out = refs[0], refs[1 : 1 + terms], refs[1 + terms]
    table, partials = refs[2 + terms : 4 + terms]
    capacity = SEC_DEV * STATES // devices
    share = capacity // terms
    js = piece_order(terms)
    me, term = lax.axis_index("sec"), lax.axis_index("term")
    source = me ^ step
    local = left.shape[2] // (ROWS // terms)
    depth = local * SECTOR

    def place(n, count):
        table[count] = n
        owner = partner[source * SEC_DEV + n // STATES, n % STATES] // SEC_DEV
        return count + jnp.where(owner == me, 1, 0)

    lax.fori_loop(0, SEC_DEV * STATES, place, 0)
    if step == 0:
        wave, (blocks, sems) = pieces[0], refs[4 + terms :]
        copies = []
        for slot in range(capacity):
            copy = pltpu.make_async_copy(wave.at[table[slot]], blocks.at[slot], sems.at[slot])
            copy.start()
            copies.append(copy)
        for copy in copies:
            copy.wait()
    row_index = lax.broadcasted_iota(jnp.int32, (SECTOR, SECTOR), 0)
    col_index = lax.broadcasted_iota(jnp.int32, (SECTOR, SECTOR), 1)
    group = ROWS // terms

    def slot_of(j, sub):
        return (term ^ js[j]) * share + sub

    def first(j, sub):
        slot = slot_of(j, sub)
        n = table[slot]
        sector, state = n // STATES, n % STATES
        left_id = source * SEC_DEV + sector
        left_order = order[left_id]
        right_order = order[partner[left_id, state]]
        keep = (row_index < left_order) & (col_index < right_order)
        block = blocks.at[slot] if step == 0 else pieces[j].at[sub]
        vectors = [
            jnp.where(keep, block[v].astype(jnp.float32), 0.0).astype(jnp.bfloat16)
            for v in range(2)
        ]
        both = jnp.concatenate(vectors, axis=1)
        place_row = pl.multiple_of((j * share + sub) * 2 * group, 2 * group)
        for i in range(terms):
            origin = term ^ js[i]
            product = jnp.dot(left[origin, sector], both, preferred_element_type=jnp.float32)
            for t in range(local):
                rows = product[t * group : (t + 1) * group]
                pair = jnp.concatenate([rows[:, :SECTOR], rows[:, SECTOR:]], axis=0)
                pair = pair * coef[origin * local + t, state]
                start = (i * local + t) * SECTOR
                partials[pl.ds(place_row, 2 * group), start : start + SECTOR] = pair.astype(
                    jnp.bfloat16
                )

    for j in range(terms):

        def inner(sub, carry, j=j):
            first(j, sub)
            return carry

        lax.fori_loop(0, share, inner, 0)

    total = jnp.zeros((capacity * 2 * group, SEC_DEV * SECTOR), jnp.float32)
    for i in range(terms):
        right = [rights[i][p].reshape(depth, SECTOR) for p in range(SEC_DEV)]
        total = total + jnp.dot(
            partials[:, i * depth : (i + 1) * depth],
            jnp.concatenate(right, axis=1),
            preferred_element_type=jnp.float32,
        )
    column = lax.broadcasted_iota(jnp.int32, (2 * group, SECTOR), 1)
    for j in range(terms):
        for sub in range(share):
            slot = slot_of(j, sub)
            n = table[slot]
            right_id = partner[source * SEC_DEV + n // STATES, n % STATES]
            start = (j * share + sub) * 2 * group
            mine = total[start : start + 2 * group]
            result = mine[:, :SECTOR]
            for p in range(1, SEC_DEV):
                result = jnp.where(
                    right_id % SEC_DEV == p, mine[:, p * SECTOR : (p + 1) * SECTOR], result
                )
            result = jnp.where(column < order[right_id], result, 0.0)
            for v in range(2):
                out[slot, v] = result[v * group : (v + 1) * group].astype(jnp.bfloat16)


def compute(step, pieces, left, rights, coef, order, partner, devices, terms):
    capacity = SEC_DEV * STATES // devices
    group = ROWS // terms
    local = left.shape[2] // group
    scratch = [
        pltpu.SMEM((SEC_DEV * STATES + 1,), jnp.int32),
        pltpu.VMEM((capacity * 2 * group, terms * local * SECTOR), jnp.bfloat16),
    ]
    if step == 0:
        scratch += [
            pltpu.VMEM((capacity, 2, SECTOR, SECTOR), jnp.bfloat16),
            pltpu.SemaphoreType.DMA((capacity,)),
        ]
    return pl.pallas_call(
        functools.partial(compute_kernel, step, devices, terms),
        out_shape=jax.ShapeDtypeStruct((capacity, 2, group, SECTOR), jnp.bfloat16),
        in_specs=[SMEM] * 3 + [ANY if step == 0 else VMEM] * len(pieces) + [VMEM] * (1 + terms),
        out_specs=VMEM,
        scratch_shapes=scratch,
        compiler_params=pltpu.CompilerParams(vmem_limit_bytes=32 << 20),
        cost_estimate=pl.CostEstimate(
            flops=3 << 30, bytes_accessed=4 << 20, transcendentals=0
        ),
        name=f"products_{step}",
    )(partner, order, coef, *pieces, left, *rights)


def unpack_kernel(devices, partner, *refs):
    chunks, out, counts = refs[:devices], refs[devices], refs[devices + 1]
    me = lax.axis_index("sec")
    for owner in range(devices):
        counts[owner] = 0

    def place(n, carry):
        owner = partner[me * SEC_DEV + n // STATES, n % STATES] // SEC_DEV
        rank = counts[owner]
        counts[owner] = rank + 1
        for step in range(devices):

            @pl.when((me ^ step) == owner)
            def _():
                out[n] = chunks[step][rank]

        return carry

    lax.fori_loop(0, SEC_DEV * STATES, place, 0)


def unpack(chunks, partner, devices):
    return pl.pallas_call(
        functools.partial(unpack_kernel, devices),
        out_shape=jax.ShapeDtypeStruct((SEC_DEV * STATES,) + chunks[0].shape[1:], jnp.bfloat16),
        in_specs=[SMEM] + [VMEM] * devices,
        out_specs=VMEM,
        scratch_shapes=[pltpu.SMEM((devices,), jnp.int32)],
        cost_estimate=pl.CostEstimate(flops=0, bytes_accessed=1 << 20, transcendentals=0),
        name="unpack",
    )(partner, *chunks)


def paired_body(wavefunction, left_window, right_blocks, couplings, sector_order, partner):
    devices, terms = lax.axis_size("sec"), lax.axis_size("term")
    block_count = SEC_DEV * STATES
    wave = wavefunction.reshape(block_count, 2, SECTOR, SECTOR)
    steps = list(range(devices - 1, 0, -1))
    coef = lax.all_gather(couplings, "term", axis=0, tiled=True)
    rights = gather_pieces(right_blocks, "term")
    sends, left_cut = pack(wave, left_window, partner, devices, terms)
    arrived = {step: exchange(sends[step - 1], "sec", step) for step in steps}
    left_all = lax.all_to_all(left_cut, "term", split_axis=0, concat_axis=0, tiled=True)
    lefts = {step: exchange(left_all, "sec", step) for step in steps}
    lefts[0] = left_all
    vectors = {step: gather_pieces(arrived[step], "term") for step in steps}
    vectors[0] = [wave]
    results = {
        step: compute(
            step, vectors[step], lefts[step], rights, coef, sector_order, partner, devices, terms
        )
        for step in [0] + steps
    }
    chunks = [results[0]] + [exchange(results[step], "sec", step) for step in range(1, devices)]
    out = unpack(chunks, partner, devices)
    return out.reshape(SEC_DEV, STATES, 2, ROWS // terms, SECTOR)


def power_of_two(number):
    return number & (number - 1) == 0


def solution(mesh):
    in_specs = (
        P(("grp", "sec"), None, None, None, None),
        P(("grp", "sec"), "term", None, None),
        P(("grp", "sec"), "term", None, None),
        P("term", None),
        P("grp"),
        P("grp", None),
    )
    out_specs = P(("grp", "sec"), None, None, "term", None)
    devices, terms = mesh.shape["sec"], mesh.shape["term"]
    paired = (
        power_of_two(devices)
        and power_of_two(terms)
        and devices <= 8
        and SEC_DEV * STATES % (devices * terms) == 0
        and ROWS == 8 * terms
    )
    body = paired_body if paired else general_body
    return jax.shard_map(body, mesh=mesh, in_specs=in_specs, out_specs=out_specs, check_vma=False)
```

```python
import functools
import math

import jax
import jax.numpy as jnp
from jax import lax
from jax.experimental import pallas as pl
from jax.experimental.pallas import tpu as pltpu
from jax.sharding import PartitionSpec as P

SECTOR = 128
STATES = 16
ROWS = 32
SEC_DEV = 2
NEAR = 2
RETURNED = jnp.bfloat16


def lookup(values_table, indices):
    columns = jnp.arange(values_table.shape[0], dtype=jnp.int32)
    matched = (indices[..., None] == columns).astype(jnp.int32)
    return jnp.sum(matched * values_table, axis=-1)


def general_body(wavefunction, left_window, right_blocks, couplings, sector_order, partner):
    devices = lax.axis_size("sec")
    myself = lax.axis_index("sec")
    block_count = SEC_DEV * STATES
    capacity = max(1, block_count // devices)
    slot_count = devices * capacity
    term_local = left_window.shape[1]
    column_index = jnp.arange(SECTOR, dtype=jnp.int32)
    positions = jnp.arange(block_count, dtype=jnp.int32)
    partner_all = partner.reshape(devices, block_count)
    owner_all = partner_all // SEC_DEV
    earlier = positions[None, :] < positions[:, None]
    same_owner = owner_all[:, :, None] == owner_all[:, None, :]
    rank_all = jnp.sum((same_owner & earlier[None]).astype(jnp.int32), axis=2)
    own_owner = lax.dynamic_index_in_dim(owner_all, myself, 0, keepdims=False)
    own_rank = lax.dynamic_index_in_dim(rank_all, myself, 0, keepdims=False)
    own_partner = lax.dynamic_index_in_dim(partner_all, myself, 0, keepdims=False)
    send_slot = own_owner * capacity + own_rank
    slot_index = jnp.arange(capacity, dtype=jnp.int32)
    matches = (owner_all == myself)[:, :, None] & (
        rank_all[:, :, None] == slot_index[None, None, :]
    )
    hit_int = matches.astype(jnp.int32)
    incoming_partner = jnp.sum(hit_int * partner_all[:, :, None], axis=1).reshape(slot_count)
    incoming_state = jnp.sum(hit_int * (positions % STATES)[None, :, None], axis=1).reshape(
        slot_count
    )
    incoming_local = incoming_partner % SEC_DEV
    incoming_order = lookup(sector_order, incoming_partner)
    column_mask = (column_index[None, :] < incoming_order[:, None]).astype(jnp.float32)
    left_order = lax.dynamic_slice_in_dim(sector_order, myself * SEC_DEV, SEC_DEV)
    right_order = lookup(sector_order, own_partner).reshape(SEC_DEV, STATES)
    row_keep = column_index[None, :] < left_order[:, None]
    col_keep = column_index[None, None, :] < right_order[:, :, None]
    keep_mask = (row_keep[:, None, None, :, None] & col_keep[:, :, None, None, :]).astype(
        jnp.bfloat16
    )
    masked = wavefunction * keep_mask
    groups = math.gcd(slot_count, 8)
    per_group = slot_count // groups

    def right_product(partials, chosen, mask_rows):
        picked = jnp.take(right_blocks, chosen, axis=0)
        result = jnp.einsum(
            "gvtrn,gtnk->gvrk", partials, picked, preferred_element_type=jnp.float32
        )
        return result * mask_rows[:, None, None, :]

    vectors = masked.reshape(block_count, 2, SECTOR, SECTOR)
    left_rows = jnp.take(left_window, positions // STATES, axis=0)
    vector_slots = (
        jnp.zeros((slot_count, 2, SECTOR, SECTOR), jnp.bfloat16).at[send_slot].set(vectors)
    )
    row_slots = (
        jnp.zeros((slot_count, term_local, ROWS, SECTOR), jnp.bfloat16).at[send_slot].set(left_rows)
    )
    vector_in, rows_in = (
        lax.all_to_all(vector_slots, "sec", split_axis=0, concat_axis=0, tiled=True),
        lax.all_to_all(row_slots, "sec", split_axis=0, concat_axis=0, tiled=True),
    )
    slot_coupling = jnp.transpose(jnp.take(couplings, incoming_state, axis=1))

    def grouped_both(inputs):
        vector_group, rows_group, coupling_group, chosen_group, mask_group = inputs
        partials = jnp.einsum(
            "gtrn,gvnj->gvtrj", rows_group, vector_group, preferred_element_type=jnp.float32
        )
        partials = (partials * coupling_group[:, None, :, None, None]).astype(jnp.bfloat16)
        return right_product(partials, chosen_group, mask_group)

    outcome = lax.map(
        grouped_both,
        (
            vector_in.reshape(groups, per_group, 2, SECTOR, SECTOR),
            rows_in.reshape(groups, per_group, term_local, ROWS, SECTOR),
            slot_coupling.reshape(groups, per_group, term_local),
            incoming_local.reshape(groups, per_group),
            column_mask.reshape(groups, per_group, SECTOR),
        ),
    )
    outcome = outcome.reshape(slot_count, 2, ROWS, SECTOR)
    returned_rows = lax.all_to_all(outcome, "sec", split_axis=0, concat_axis=0, tiled=True)
    own_rows = jnp.take(returned_rows, send_slot, axis=0).reshape(SEC_DEV, STATES, 2, ROWS, SECTOR)
    summed = lax.psum_scatter(own_rows, "term", scatter_dimension=3, tiled=True)
    return summed.astype(jnp.bfloat16)


def after(value, *earlier):
    return lax.optimization_barrier((value,) + earlier)[0]


def partner_of(partner, device, n):
    return partner[device * SEC_DEV + lax.shift_right_logical(n, 4), n & (STATES - 1)]


def owner_of(sector):
    return lax.shift_right_logical(sector, 1)


ANY = pl.BlockSpec(memory_space=pl.ANY)
VMEM = pl.BlockSpec(memory_space=pltpu.VMEM)
SMEM = pl.BlockSpec(memory_space=pltpu.SMEM)


def exchange(x, axis, step):
    size = lax.axis_size(axis)
    return lax.ppermute(x, axis, [(i, i ^ step) for i in range(size)])


def exchange_both(x, step, term_step):
    devices, terms = lax.axis_size("sec"), lax.axis_size("term")
    if step == 0:
        return exchange(x, "term", term_step)
    pairs = [
        (s * terms + t, (s ^ step) * terms + (t ^ term_step))
        for s in range(devices)
        for t in range(terms)
    ]
    return lax.ppermute(x, ("sec", "term"), pairs)


def piece_order(size):
    order = [0]
    bit = size // 2
    while bit:
        order = order + [j ^ bit for j in order]
        bit //= 2
    return order


def pack_kernel(devices, terms, partner, wave, left, *refs):
    sends = refs[: devices - 1]
    keep, give, counts, table, sems = refs[devices - 1 :]
    capacity = SEC_DEV * STATES // devices
    share = capacity // terms
    me, term = lax.axis_index("sec"), lax.axis_index("term")
    for owner in range(devices):
        counts[owner] = 0

    def place(n, carry):
        owner = owner_of(partner_of(partner, me, n))
        rank = counts[owner]
        counts[owner] = rank + 1
        table[owner * capacity + rank] = n
        return carry

    lax.fori_loop(0, SEC_DEV * STATES, place, 0, unroll=True)
    copies = []
    for step in range(1, devices):
        target = me ^ step
        for sub in range(share):
            n = table[target * capacity + term * share + sub]
            copy = pltpu.make_async_copy(
                wave.at[n], sends[step - 1].at[sub], sems.at[(step - 1) * share + sub]
            )
            copy.start()
            copies.append(copy)
    group = ROWS // terms
    first_core = (term & (NEAR - 1)) == 0
    for a in range(SEC_DEV):
        for t in range(left.shape[1]):
            rows = left[a, t].astype(jnp.float32)
            tiles = [
                jnp.concatenate(
                    [
                        rows[(far * NEAR + near) * group : (far * NEAR + near + 1) * group]
                        for far in range(terms // NEAR)
                    ],
                    axis=0,
                )
                for near in range(NEAR)
            ]
            place_rows = slice(t * 2 * group, (t + 1) * 2 * group)
            keep[a, place_rows, :] = jnp.where(first_core, tiles[0], tiles[1]).astype(jnp.bfloat16)
            give[a, place_rows, :] = jnp.where(first_core, tiles[1], tiles[0]).astype(jnp.bfloat16)
    for copy in copies:
        copy.wait()


def pack(wave, left, partner, devices, terms):
    capacity = SEC_DEV * STATES // devices
    share = capacity // terms
    local = left.shape[1]
    piece = jax.ShapeDtypeStruct((share, 2, SECTOR, SECTOR), jnp.bfloat16)
    rows = jax.ShapeDtypeStruct((SEC_DEV, local * (ROWS // NEAR), SECTOR), jnp.bfloat16)
    outs = pl.pallas_call(
        functools.partial(pack_kernel, devices, terms),
        out_shape=[piece] * (devices - 1) + [rows] * 2,
        in_specs=[SMEM, ANY, VMEM],
        out_specs=[VMEM] * (devices + 1),
        scratch_shapes=[
            pltpu.SMEM((devices,), jnp.int32),
            pltpu.SMEM((SEC_DEV * STATES,), jnp.int32),
            pltpu.SemaphoreType.DMA(((devices - 1) * share,)),
        ],
        cost_estimate=pl.CostEstimate(flops=0, bytes_accessed=4 << 20, transcendentals=0),
        name="pack",
    )(partner, wave, left)
    return outs[: devices - 1], outs[devices - 1], outs[devices]


def compute_kernel(step, devices, terms, partner, order, *refs):
    coefs, refs = refs[:NEAR], refs[NEAR:]
    pieces = refs[: 1 if step == 0 else terms]
    refs = refs[len(pieces) :]
    left, rights, (keep, give) = refs[0], refs[1 : 1 + NEAR], refs[1 + NEAR : 3 + NEAR]
    table, partials = refs[3 + NEAR : 5 + NEAR]
    capacity = SEC_DEV * STATES // devices
    share = capacity // terms
    js = piece_order(terms)
    me, term = lax.axis_index("sec"), lax.axis_index("term")
    source = me ^ step
    group = ROWS // terms
    rows = ROWS // NEAR
    local = left.shape[2] // rows
    depth = local * SECTOR

    def place(n, count):
        table[count] = n
        owner = owner_of(partner_of(partner, source, n))
        return count + jnp.where(owner == me, 1, 0)

    lax.fori_loop(0, SEC_DEV * STATES, place, 0, unroll=True)
    if step == 0:
        wave, (blocks, sems) = pieces[0], refs[5 + NEAR :]
        copies = []
        for slot in range(capacity):
            copy = pltpu.make_async_copy(wave.at[table[slot]], blocks.at[slot], sems.at[slot])
            copy.start()
            copies.append(copy)
        for copy in copies:
            copy.wait()
    row_index = lax.broadcasted_iota(jnp.int32, (SECTOR, SECTOR), 0)
    col_index = lax.broadcasted_iota(jnp.int32, (SECTOR, SECTOR), 1)

    def slot_of(j, sub):
        return (term ^ js[j]) * share + sub

    def first(j, sub):
        slot = slot_of(j, sub)
        n = table[slot]
        sector, state = lax.shift_right_logical(n, 4), n & (STATES - 1)
        left_order = order[source * SEC_DEV + sector]
        right_order = order[partner_of(partner, source, n)]
        keep_mask = (row_index < left_order) & (col_index < right_order)
        block = blocks.at[slot] if step == 0 else pieces[j].at[sub]
        vectors = [
            jnp.where(keep_mask, block[v].astype(jnp.float32), 0.0).astype(jnp.bfloat16)
            for v in range(2)
        ]
        both = jnp.concatenate(vectors, axis=1)
        place_row = (j * share + sub) * 2 * rows
        for i in range(NEAR):
            product = jnp.dot(left[i, sector], both, preferred_element_type=jnp.float32)
            for t in range(local):
                scaled = product[t * rows : (t + 1) * rows] * coefs[i][t, state]
                start = (i * local + t) * SECTOR
                for v in range(2):
                    partials[
                        place_row + v * rows : place_row + (v + 1) * rows, start : start + SECTOR
                    ] = scaled[:, v * SECTOR : (v + 1) * SECTOR].astype(jnp.bfloat16)

    for j in range(terms):
        for sub in range(share):
            first(j, sub)

    total = jnp.zeros((capacity * 2 * rows, SEC_DEV * SECTOR), jnp.float32)
    for i in range(NEAR):
        right = [rights[i][p].reshape(depth, SECTOR) for p in range(SEC_DEV)]
        total = total + jnp.dot(
            partials[:, i * depth : (i + 1) * depth],
            jnp.concatenate(right, axis=1),
            preferred_element_type=jnp.float32,
        )
    column = lax.broadcasted_iota(jnp.int32, (2 * rows, SECTOR), 1)
    near_first = term < NEAR
    for j in range(terms):
        for sub in range(share):
            slot = slot_of(j, sub)
            n = table[slot]
            right_id = partner_of(partner, source, n)
            start = (j * share + sub) * 2 * rows
            mine = total[start : start + 2 * rows]
            result = mine[:, :SECTOR]
            for p in range(1, SEC_DEV):
                result = jnp.where(
                    (right_id & (SEC_DEV - 1)) == p, mine[:, p * SECTOR : (p + 1) * SECTOR], result
                )
            result = jnp.where(column < order[right_id], result, 0.0)
            for v in range(2):
                low = result[v * rows : v * rows + group]
                high = result[v * rows + group : (v + 1) * rows]
                keep[slot, v] = jnp.where(near_first, low, high).astype(keep.dtype)
                give[slot, v] = jnp.where(near_first, high, low).astype(give.dtype)


def compute(step, pieces, left, rights, coefs, order, partner, devices, terms):
    capacity = SEC_DEV * STATES // devices
    rows = ROWS // NEAR
    local = left.shape[2] // rows
    scratch = [
        pltpu.SMEM((SEC_DEV * STATES + 1,), jnp.int32),
        pltpu.VMEM((capacity * 2 * rows, NEAR * local * SECTOR), jnp.bfloat16),
    ]
    if step == 0:
        scratch += [
            pltpu.VMEM((capacity, 2, SECTOR, SECTOR), jnp.bfloat16),
            pltpu.SemaphoreType.DMA((capacity,)),
        ]
    part = jax.ShapeDtypeStruct((capacity, 2, ROWS // terms, SECTOR), RETURNED)
    return pl.pallas_call(
        functools.partial(compute_kernel, step, devices, terms),
        out_shape=[part, part],
        in_specs=[SMEM] * (2 + NEAR)
        + [ANY if step == 0 else VMEM] * len(pieces)
        + [VMEM] * (1 + NEAR),
        out_specs=[VMEM, VMEM],
        scratch_shapes=scratch,
        compiler_params=pltpu.CompilerParams(vmem_limit_bytes=32 << 20),
        cost_estimate=pl.CostEstimate(
            flops=3 << 30, bytes_accessed=4 << 20, transcendentals=0
        ),
        name=f"products_{step}",
    )(partner, order, *coefs, *pieces, left, *rights)


def unpack_kernel(devices, partner, *refs):
    chunks, (out, held, counts, table, sems) = refs[: 2 * devices], refs[2 * devices :]
    capacity = SEC_DEV * STATES // devices
    me = lax.axis_index("sec")
    copies = []
    for i in range(2 * devices):
        copy = pltpu.make_async_copy(chunks[i], held.at[i], sems.at[i])
        copy.start()
        copies.append(copy)
    for owner in range(devices):
        counts[owner] = 0

    def place(n, carry):
        owner = owner_of(partner_of(partner, me, n))
        rank = counts[owner]
        counts[owner] = rank + 1
        table[owner * capacity + rank] = n
        return carry

    lax.fori_loop(0, SEC_DEV * STATES, place, 0, unroll=True)
    for copy in copies:
        copy.wait()
    for step in range(devices):
        for rank in range(capacity):
            near = held[2 * step, rank].astype(jnp.float32)
            far = held[2 * step + 1, rank].astype(jnp.float32)
            out[table[(me ^ step) * capacity + rank]] = (near + far).astype(jnp.bfloat16)


def unpack(chunks, partner, devices):
    return pl.pallas_call(
        functools.partial(unpack_kernel, devices),
        out_shape=jax.ShapeDtypeStruct((SEC_DEV * STATES,) + chunks[0].shape[1:], jnp.bfloat16),
        in_specs=[SMEM] + [ANY] * (2 * devices),
        out_specs=VMEM,
        scratch_shapes=[
            pltpu.VMEM((2 * devices,) + chunks[0].shape, RETURNED),
            pltpu.SMEM((devices,), jnp.int32),
            pltpu.SMEM((SEC_DEV * STATES,), jnp.int32),
            pltpu.SemaphoreType.DMA((2 * devices,)),
        ],
        cost_estimate=pl.CostEstimate(flops=0, bytes_accessed=1 << 20, transcendentals=0),
        name="unpack",
    )(partner, *chunks)


def paired_body(wavefunction, left_window, right_blocks, couplings, sector_order, partner):
    devices, terms = lax.axis_size("sec"), lax.axis_size("term")
    block_count = SEC_DEV * STATES
    wave = wavefunction.reshape(block_count, 2, SECTOR, SECTOR)
    steps = list(range(devices - 1, 0, -1))
    sends, left_keep, left_give = pack(wave, left_window, partner, devices, terms)
    coefs = [couplings, exchange(couplings, "term", 1)]
    rights = [right_blocks, exchange(right_blocks, "term", 1)]
    left_all = jnp.stack([left_keep, exchange(left_give, "term", 1)])
    arrived = {step: exchange(sends[step - 1], "sec", step) for step in steps}
    lefts = {step: exchange(left_all, "sec", step) for step in steps}
    lefts[0] = left_all
    vectors = {0: [wave]}
    for step in steps:
        x = exchange(arrived[step], "term", NEAR)
        both = jnp.concatenate([arrived[step], x])
        both = jnp.concatenate([both, exchange(both, "term", 1)])
        vectors[step] = jnp.split(both, terms)
    chunks = {}
    waits = []
    for step in [0] + steps:
        keep, give = compute(
            step,
            vectors[step],
            after(lefts[step], *waits),
            rights,
            coefs,
            sector_order,
            partner,
            devices,
            terms,
        )
        waits = [keep] + [part for value in list(chunks.values())[-1:] for part in value]
        if step:
            keep = exchange(keep, "sec", step)
        chunks[step] = (keep, exchange_both(give, step, NEAR))
    chunks = [part for step in range(devices) for part in chunks[step]]
    out = unpack(chunks, partner, devices)
    return out.reshape(SEC_DEV, STATES, 2, ROWS // terms, SECTOR)


def power_of_two(number):
    return number & (number - 1) == 0


def solution(mesh):
    in_specs = (
        P(("grp", "sec"), None, None, None, None),
        P(("grp", "sec"), "term", None, None),
        P(("grp", "sec"), "term", None, None),
        P("term", None),
        P("grp"),
        P("grp", None),
    )
    out_specs = P(("grp", "sec"), None, None, "term", None)
    devices, terms = mesh.shape["sec"], mesh.shape["term"]
    paired = (
        power_of_two(devices)
        and terms == 2 * NEAR
        and devices <= 8
        and SEC_DEV * STATES % (devices * terms) == 0
        and ROWS == 8 * terms
    )
    body = paired_body if paired else general_body
    return jax.shard_map(body, mesh=mesh, in_specs=in_specs, out_specs=out_specs, check_vma=False)
```

```python
import functools
import math

import jax
import jax.numpy as jnp
from jax import lax
from jax.experimental import pallas as pl
from jax.experimental.pallas import tpu as pltpu
from jax.sharding import PartitionSpec as P

SECTOR = 128
STATES = 16
ROWS = 32
SEC_DEV = 2
NEAR = 2
RETURNED = jnp.bfloat16


def lookup(values_table, indices):
    columns = jnp.arange(values_table.shape[0], dtype=jnp.int32)
    matched = (indices[..., None] == columns).astype(jnp.int32)
    return jnp.sum(matched * values_table, axis=-1)


def general_body(wavefunction, left_window, right_blocks, couplings, sector_order, partner):
    devices = lax.axis_size("sec")
    myself = lax.axis_index("sec")
    block_count = SEC_DEV * STATES
    capacity = max(1, block_count // devices)
    slot_count = devices * capacity
    term_local = left_window.shape[1]
    column_index = jnp.arange(SECTOR, dtype=jnp.int32)
    positions = jnp.arange(block_count, dtype=jnp.int32)
    partner_all = partner.reshape(devices, block_count)
    owner_all = partner_all // SEC_DEV
    earlier = positions[None, :] < positions[:, None]
    same_owner = owner_all[:, :, None] == owner_all[:, None, :]
    rank_all = jnp.sum((same_owner & earlier[None]).astype(jnp.int32), axis=2)
    own_owner = lax.dynamic_index_in_dim(owner_all, myself, 0, keepdims=False)
    own_rank = lax.dynamic_index_in_dim(rank_all, myself, 0, keepdims=False)
    own_partner = lax.dynamic_index_in_dim(partner_all, myself, 0, keepdims=False)
    send_slot = own_owner * capacity + own_rank
    slot_index = jnp.arange(capacity, dtype=jnp.int32)
    matches = (owner_all == myself)[:, :, None] & (
        rank_all[:, :, None] == slot_index[None, None, :]
    )
    hit_int = matches.astype(jnp.int32)
    incoming_partner = jnp.sum(hit_int * partner_all[:, :, None], axis=1).reshape(slot_count)
    incoming_state = jnp.sum(hit_int * (positions % STATES)[None, :, None], axis=1).reshape(
        slot_count
    )
    incoming_local = incoming_partner % SEC_DEV
    incoming_order = lookup(sector_order, incoming_partner)
    column_mask = (column_index[None, :] < incoming_order[:, None]).astype(jnp.float32)
    left_order = lax.dynamic_slice_in_dim(sector_order, myself * SEC_DEV, SEC_DEV)
    right_order = lookup(sector_order, own_partner).reshape(SEC_DEV, STATES)
    row_keep = column_index[None, :] < left_order[:, None]
    col_keep = column_index[None, None, :] < right_order[:, :, None]
    keep_mask = (row_keep[:, None, None, :, None] & col_keep[:, :, None, None, :]).astype(
        jnp.bfloat16
    )
    masked = wavefunction * keep_mask
    groups = math.gcd(slot_count, 8)
    per_group = slot_count // groups

    def right_product(partials, chosen, mask_rows):
        picked = jnp.take(right_blocks, chosen, axis=0)
        result = jnp.einsum(
            "gvtrn,gtnk->gvrk", partials, picked, preferred_element_type=jnp.float32
        )
        return result * mask_rows[:, None, None, :]

    vectors = masked.reshape(block_count, 2, SECTOR, SECTOR)
    left_rows = jnp.take(left_window, positions // STATES, axis=0)
    vector_slots = (
        jnp.zeros((slot_count, 2, SECTOR, SECTOR), jnp.bfloat16).at[send_slot].set(vectors)
    )
    row_slots = (
        jnp.zeros((slot_count, term_local, ROWS, SECTOR), jnp.bfloat16).at[send_slot].set(left_rows)
    )
    vector_in, rows_in = (
        lax.all_to_all(vector_slots, "sec", split_axis=0, concat_axis=0, tiled=True),
        lax.all_to_all(row_slots, "sec", split_axis=0, concat_axis=0, tiled=True),
    )
    slot_coupling = jnp.transpose(jnp.take(couplings, incoming_state, axis=1))

    def grouped_both(inputs):
        vector_group, rows_group, coupling_group, chosen_group, mask_group = inputs
        partials = jnp.einsum(
            "gtrn,gvnj->gvtrj", rows_group, vector_group, preferred_element_type=jnp.float32
        )
        partials = (partials * coupling_group[:, None, :, None, None]).astype(jnp.bfloat16)
        return right_product(partials, chosen_group, mask_group)

    outcome = lax.map(
        grouped_both,
        (
            vector_in.reshape(groups, per_group, 2, SECTOR, SECTOR),
            rows_in.reshape(groups, per_group, term_local, ROWS, SECTOR),
            slot_coupling.reshape(groups, per_group, term_local),
            incoming_local.reshape(groups, per_group),
            column_mask.reshape(groups, per_group, SECTOR),
        ),
    )
    outcome = outcome.reshape(slot_count, 2, ROWS, SECTOR)
    returned_rows = lax.all_to_all(outcome, "sec", split_axis=0, concat_axis=0, tiled=True)
    own_rows = jnp.take(returned_rows, send_slot, axis=0).reshape(SEC_DEV, STATES, 2, ROWS, SECTOR)
    summed = lax.psum_scatter(own_rows, "term", scatter_dimension=3, tiled=True)
    return summed.astype(jnp.bfloat16)


def after(value, *earlier):
    return lax.optimization_barrier((value,) + earlier)[0]


def partner_of(partner, device, n):
    return partner[device * SEC_DEV + lax.shift_right_logical(n, 4), n & (STATES - 1)]


def owner_of(sector):
    return lax.shift_right_logical(sector, 1)


ANY = pl.BlockSpec(memory_space=pl.ANY)
VMEM = pl.BlockSpec(memory_space=pltpu.VMEM)
SMEM = pl.BlockSpec(memory_space=pltpu.SMEM)


def exchange(x, axis, step):
    size = lax.axis_size(axis)
    return lax.ppermute(x, axis, [(i, i ^ step) for i in range(size)])


def exchange_both(x, step, term_step):
    devices, terms = lax.axis_size("sec"), lax.axis_size("term")
    if step == 0:
        return exchange(x, "term", term_step)
    pairs = [
        (s * terms + t, (s ^ step) * terms + (t ^ term_step))
        for s in range(devices)
        for t in range(terms)
    ]
    return lax.ppermute(x, ("sec", "term"), pairs)


def piece_order(size):
    order = [0]
    bit = size // 2
    while bit:
        order = order + [j ^ bit for j in order]
        bit //= 2
    return order


def pack_kernel(devices, terms, partner, wave, *refs):
    sends = refs[: devices - 1]
    counts, table, sems = refs[devices - 1 :]
    capacity = SEC_DEV * STATES // devices
    share = capacity // terms
    me, term = lax.axis_index("sec"), lax.axis_index("term")
    for owner in range(devices):
        counts[owner] = 0

    def place(n, carry):
        owner = owner_of(partner_of(partner, me, n))
        rank = counts[owner]
        counts[owner] = rank + 1
        table[owner * capacity + rank] = n
        return carry

    lax.fori_loop(0, SEC_DEV * STATES, place, 0, unroll=True)
    copies = []
    for step in range(1, devices):
        target = me ^ step
        for sub in range(share):
            n = table[target * capacity + term * share + sub]
            copy = pltpu.make_async_copy(
                wave.at[n], sends[step - 1].at[sub], sems.at[(step - 1) * share + sub]
            )
            copy.start()
            copies.append(copy)
    for copy in copies:
        copy.wait()


def pack(wave, partner, devices, terms):
    capacity = SEC_DEV * STATES // devices
    share = capacity // terms
    piece = jax.ShapeDtypeStruct((share, 2, SECTOR, SECTOR), jnp.bfloat16)
    return pl.pallas_call(
        functools.partial(pack_kernel, devices, terms),
        out_shape=[piece] * (devices - 1),
        in_specs=[SMEM, ANY],
        out_specs=[VMEM] * (devices - 1),
        scratch_shapes=[
            pltpu.SMEM((devices,), jnp.int32),
            pltpu.SMEM((SEC_DEV * STATES,), jnp.int32),
            pltpu.SemaphoreType.DMA(((devices - 1) * share,)),
        ],
        cost_estimate=pl.CostEstimate(flops=0, bytes_accessed=4 << 20, transcendentals=0),
        name="pack",
    )(partner, wave)


def compute_kernel(step, devices, terms, partner, order, *refs):
    coefs, refs = refs[:NEAR], refs[NEAR:]
    pieces = refs[: 1 if step == 0 else terms]
    refs = refs[len(pieces) :]
    lefts, refs = refs[:NEAR], refs[NEAR:]
    rights, (keep, give) = refs[:NEAR], refs[NEAR : 2 + NEAR]
    table, partials, cut = refs[2 + NEAR : 5 + NEAR]
    capacity = SEC_DEV * STATES // devices
    share = capacity // terms
    js = piece_order(terms)
    me, term = lax.axis_index("sec"), lax.axis_index("term")
    source = me ^ step
    group = ROWS // terms
    rows = ROWS // NEAR
    local = lefts[0].shape[1]
    depth = local * SECTOR

    def place(n, count):
        table[count] = n
        owner = owner_of(partner_of(partner, source, n))
        return count + jnp.where(owner == me, 1, 0)

    lax.fori_loop(0, SEC_DEV * STATES, place, 0, unroll=True)
    if step == 0:
        wave, (blocks, sems) = pieces[0], refs[5 + NEAR :]
        copies = []
        for slot in range(capacity):
            copy = pltpu.make_async_copy(wave.at[table[slot]], blocks.at[slot], sems.at[slot])
            copy.start()
            copies.append(copy)
        for copy in copies:
            copy.wait()
    first_core = (term & (NEAR - 1)) == 0
    for i in range(NEAR):
        for a in range(SEC_DEV):
            for t in range(local):
                whole = lefts[i][a, t].astype(jnp.float32)
                parts = [whole[r * group : (r + 1) * group] for r in range(terms)]
                tile = jnp.concatenate(
                    [jnp.where(first_core, parts[r], parts[r + 1]) for r in range(0, terms, NEAR)],
                    axis=0,
                )
                cut[i, a, t * rows : (t + 1) * rows, :] = tile.astype(jnp.bfloat16)
    row_index = lax.broadcasted_iota(jnp.int32, (SECTOR, SECTOR), 0)
    col_index = lax.broadcasted_iota(jnp.int32, (SECTOR, SECTOR), 1)

    def slot_of(j, sub):
        return (term ^ js[j]) * share + sub

    def first(j, sub):
        slot = slot_of(j, sub)
        n = table[slot]
        sector, state = lax.shift_right_logical(n, 4), n & (STATES - 1)
        left_order = order[source * SEC_DEV + sector]
        right_order = order[partner_of(partner, source, n)]
        keep_mask = (row_index < left_order) & (col_index < right_order)
        block = blocks.at[slot] if step == 0 else pieces[j].at[sub]
        vectors = [
            jnp.where(keep_mask, block[v].astype(jnp.float32), 0.0).astype(jnp.bfloat16)
            for v in range(2)
        ]
        both = jnp.concatenate(vectors, axis=1)
        place_row = (j * share + sub) * 2 * rows
        for i in range(NEAR):
            product = jnp.dot(cut[i, sector], both, preferred_element_type=jnp.float32)
            for t in range(local):
                scaled = product[t * rows : (t + 1) * rows] * coefs[i][t, state]
                start = (i * local + t) * SECTOR
                for v in range(2):
                    partials[
                        place_row + v * rows : place_row + (v + 1) * rows, start : start + SECTOR
                    ] = scaled[:, v * SECTOR : (v + 1) * SECTOR].astype(jnp.bfloat16)

    for j in range(terms):
        for sub in range(share):
            first(j, sub)

    total = jnp.zeros((capacity * 2 * rows, SEC_DEV * SECTOR), jnp.float32)
    for i in range(NEAR):
        right = [rights[i][p].reshape(depth, SECTOR) for p in range(SEC_DEV)]
        total = total + jnp.dot(
            partials[:, i * depth : (i + 1) * depth],
            jnp.concatenate(right, axis=1),
            preferred_element_type=jnp.float32,
        )
    column = lax.broadcasted_iota(jnp.int32, (2 * rows, SECTOR), 1)
    near_first = term < NEAR
    for j in range(terms):
        for sub in range(share):
            slot = slot_of(j, sub)
            n = table[slot]
            right_id = partner_of(partner, source, n)
            start = (j * share + sub) * 2 * rows
            mine = total[start : start + 2 * rows]
            result = mine[:, :SECTOR]
            for p in range(1, SEC_DEV):
                result = jnp.where(
                    (right_id & (SEC_DEV - 1)) == p, mine[:, p * SECTOR : (p + 1) * SECTOR], result
                )
            result = jnp.where(column < order[right_id], result, 0.0)
            for v in range(2):
                low = result[v * rows : v * rows + group]
                high = result[v * rows + group : (v + 1) * rows]
                keep[slot, v] = jnp.where(near_first, low, high).astype(keep.dtype)
                give[slot, v] = jnp.where(near_first, high, low).astype(give.dtype)


def compute(step, pieces, lefts, rights, coefs, order, partner, devices, terms):
    capacity = SEC_DEV * STATES // devices
    rows = ROWS // NEAR
    local = lefts[0].shape[1]
    scratch = [
        pltpu.SMEM((SEC_DEV * STATES + 1,), jnp.int32),
        pltpu.VMEM((capacity * 2 * rows, NEAR * local * SECTOR), jnp.bfloat16),
        pltpu.VMEM((NEAR, SEC_DEV, local * rows, SECTOR), jnp.bfloat16),
    ]
    if step == 0:
        scratch += [
            pltpu.VMEM((capacity, 2, SECTOR, SECTOR), jnp.bfloat16),
            pltpu.SemaphoreType.DMA((capacity,)),
        ]
    part = jax.ShapeDtypeStruct((capacity, 2, ROWS // terms, SECTOR), RETURNED)
    return pl.pallas_call(
        functools.partial(compute_kernel, step, devices, terms),
        out_shape=[part, part],
        in_specs=[SMEM] * (2 + NEAR)
        + [ANY if step == 0 else VMEM] * len(pieces)
        + [VMEM] * (2 * NEAR),
        out_specs=[VMEM, VMEM],
        scratch_shapes=scratch,
        compiler_params=pltpu.CompilerParams(vmem_limit_bytes=32 << 20),
        cost_estimate=pl.CostEstimate(
            flops=3 << 30, bytes_accessed=4 << 20, transcendentals=0
        ),
        name=f"products_{step}",
    )(partner, order, *coefs, *pieces, *lefts, *rights)


def unpack_kernel(devices, partner, *refs):
    chunks, (out, held, counts, table, sems) = refs[: 2 * devices], refs[2 * devices :]
    capacity = SEC_DEV * STATES // devices
    me = lax.axis_index("sec")
    copies = []
    for i in range(2 * devices):
        copy = pltpu.make_async_copy(chunks[i], held.at[i], sems.at[i])
        copy.start()
        copies.append(copy)
    for owner in range(devices):
        counts[owner] = 0

    def place(n, carry):
        owner = owner_of(partner_of(partner, me, n))
        rank = counts[owner]
        counts[owner] = rank + 1
        table[owner * capacity + rank] = n
        return carry

    lax.fori_loop(0, SEC_DEV * STATES, place, 0, unroll=True)
    for copy in copies:
        copy.wait()
    for step in range(devices):
        for rank in range(capacity):
            near = held[2 * step, rank].astype(jnp.float32)
            far = held[2 * step + 1, rank].astype(jnp.float32)
            out[table[(me ^ step) * capacity + rank]] = (near + far).astype(jnp.bfloat16)


def unpack(chunks, partner, devices):
    return pl.pallas_call(
        functools.partial(unpack_kernel, devices),
        out_shape=jax.ShapeDtypeStruct((SEC_DEV * STATES,) + chunks[0].shape[1:], jnp.bfloat16),
        in_specs=[SMEM] + [ANY] * (2 * devices),
        out_specs=VMEM,
        scratch_shapes=[
            pltpu.VMEM((2 * devices,) + chunks[0].shape, RETURNED),
            pltpu.SMEM((devices,), jnp.int32),
            pltpu.SMEM((SEC_DEV * STATES,), jnp.int32),
            pltpu.SemaphoreType.DMA((2 * devices,)),
        ],
        cost_estimate=pl.CostEstimate(flops=0, bytes_accessed=1 << 20, transcendentals=0),
        name="unpack",
    )(partner, *chunks)


def paired_body(wavefunction, left_window, right_blocks, couplings, sector_order, partner):
    devices, terms = lax.axis_size("sec"), lax.axis_size("term")
    block_count = SEC_DEV * STATES
    wave = wavefunction.reshape(block_count, 2, SECTOR, SECTOR)
    steps = [2, 3, 1]
    coefs = [couplings, exchange(couplings, "term", 1)]
    rights = [right_blocks, exchange(right_blocks, "term", 1)]
    sends = pack(wave, partner, devices, terms)
    arrived = {step: exchange(sends[step - 1], "sec", step) for step in steps}
    every = list(arrived.values())

    def products(step, vectors, lefts):
        return compute(
            step, vectors, lefts, rights, coefs, sector_order, partner, devices, terms
        )

    left_in = {}
    held = {0: after(left_window, *every)}
    bit = devices // 2
    while bit:
        for step in list(held):
            held[step ^ bit] = left_in[step ^ bit] = exchange(held[step], "sec", bit)
        bit //= 2
    keep, give = products(0, [wave], [left_window, exchange(left_window, "term", 1)])
    chunks = {0: (keep, exchange_both(give, 0, NEAR))}
    waits = [keep]
    for step in steps:
        x = exchange(after(arrived[step], *every), "term", NEAR)
        both = jnp.concatenate([arrived[step], x])
        both, left = lax.optimization_barrier((both, left_in[step], waits[0]))[:2]
        lefts = [left, exchange(left, "term", 1)]
        both = jnp.concatenate([both, exchange(both, "term", 1)])
        lefts[0] = after(lefts[0], *waits)
        keep, give = products(step, jnp.split(both, terms), lefts)
        waits = [keep] + [part for value in list(chunks.values())[-1:] for part in value]
        chunks[step] = (exchange(keep, "sec", step), exchange_both(give, step, NEAR))
    chunks = [part for step in range(devices) for part in chunks[step]]
    out = unpack(chunks, partner, devices)
    return out.reshape(SEC_DEV, STATES, 2, ROWS // terms, SECTOR)


def power_of_two(number):
    return number & (number - 1) == 0


def solution(mesh):
    in_specs = (
        P(("grp", "sec"), None, None, None, None),
        P(("grp", "sec"), "term", None, None),
        P(("grp", "sec"), "term", None, None),
        P("term", None),
        P("grp"),
        P("grp", None),
    )
    out_specs = P(("grp", "sec"), None, None, "term", None)
    devices, terms = mesh.shape["sec"], mesh.shape["term"]
    paired = (
        power_of_two(devices)
        and terms == 2 * NEAR
        and devices <= 8
        and SEC_DEV * STATES % (devices * terms) == 0
        and ROWS == 8 * terms
    )
    body = paired_body if paired else general_body
    return jax.shard_map(body, mesh=mesh, in_specs=in_specs, out_specs=out_specs, check_vma=False)
```

```python
import functools
import math

import jax
import jax.numpy as jnp
from jax import lax
from jax.experimental import pallas as pl
from jax.experimental.pallas import tpu as pltpu
from jax.sharding import PartitionSpec as P

SECTOR = 128
STATES = 16
ROWS = 32
SEC_DEV = 2
NEAR = 2
RETURNED = jnp.bfloat16


def lookup(values_table, indices):
    columns = jnp.arange(values_table.shape[0], dtype=jnp.int32)
    matched = (indices[..., None] == columns).astype(jnp.int32)
    return jnp.sum(matched * values_table, axis=-1)


def general_body(wavefunction, left_window, right_blocks, couplings, sector_order, partner):
    devices = lax.axis_size("sec")
    myself = lax.axis_index("sec")
    block_count = SEC_DEV * STATES
    capacity = max(1, block_count // devices)
    slot_count = devices * capacity
    term_local = left_window.shape[1]
    column_index = jnp.arange(SECTOR, dtype=jnp.int32)
    positions = jnp.arange(block_count, dtype=jnp.int32)
    partner_all = partner.reshape(devices, block_count)
    owner_all = partner_all // SEC_DEV
    earlier = positions[None, :] < positions[:, None]
    same_owner = owner_all[:, :, None] == owner_all[:, None, :]
    rank_all = jnp.sum((same_owner & earlier[None]).astype(jnp.int32), axis=2)
    own_owner = lax.dynamic_index_in_dim(owner_all, myself, 0, keepdims=False)
    own_rank = lax.dynamic_index_in_dim(rank_all, myself, 0, keepdims=False)
    own_partner = lax.dynamic_index_in_dim(partner_all, myself, 0, keepdims=False)
    send_slot = own_owner * capacity + own_rank
    slot_index = jnp.arange(capacity, dtype=jnp.int32)
    matches = (owner_all == myself)[:, :, None] & (
        rank_all[:, :, None] == slot_index[None, None, :]
    )
    hit_int = matches.astype(jnp.int32)
    incoming_partner = jnp.sum(hit_int * partner_all[:, :, None], axis=1).reshape(slot_count)
    incoming_state = jnp.sum(hit_int * (positions % STATES)[None, :, None], axis=1).reshape(
        slot_count
    )
    incoming_local = incoming_partner % SEC_DEV
    incoming_order = lookup(sector_order, incoming_partner)
    column_mask = (column_index[None, :] < incoming_order[:, None]).astype(jnp.float32)
    left_order = lax.dynamic_slice_in_dim(sector_order, myself * SEC_DEV, SEC_DEV)
    right_order = lookup(sector_order, own_partner).reshape(SEC_DEV, STATES)
    row_keep = column_index[None, :] < left_order[:, None]
    col_keep = column_index[None, None, :] < right_order[:, :, None]
    keep_mask = (row_keep[:, None, None, :, None] & col_keep[:, :, None, None, :]).astype(
        jnp.bfloat16
    )
    masked = wavefunction * keep_mask
    groups = math.gcd(slot_count, 8)
    per_group = slot_count // groups

    def right_product(partials, chosen, mask_rows):
        picked = jnp.take(right_blocks, chosen, axis=0)
        result = jnp.einsum(
            "gvtrn,gtnk->gvrk", partials, picked, preferred_element_type=jnp.float32
        )
        return result * mask_rows[:, None, None, :]

    vectors = masked.reshape(block_count, 2, SECTOR, SECTOR)
    left_rows = jnp.take(left_window, positions // STATES, axis=0)
    vector_slots = (
        jnp.zeros((slot_count, 2, SECTOR, SECTOR), jnp.bfloat16).at[send_slot].set(vectors)
    )
    row_slots = (
        jnp.zeros((slot_count, term_local, ROWS, SECTOR), jnp.bfloat16).at[send_slot].set(left_rows)
    )
    vector_in, rows_in = (
        lax.all_to_all(vector_slots, "sec", split_axis=0, concat_axis=0, tiled=True),
        lax.all_to_all(row_slots, "sec", split_axis=0, concat_axis=0, tiled=True),
    )
    slot_coupling = jnp.transpose(jnp.take(couplings, incoming_state, axis=1))

    def grouped_both(inputs):
        vector_group, rows_group, coupling_group, chosen_group, mask_group = inputs
        partials = jnp.einsum(
            "gtrn,gvnj->gvtrj", rows_group, vector_group, preferred_element_type=jnp.float32
        )
        partials = (partials * coupling_group[:, None, :, None, None]).astype(jnp.bfloat16)
        return right_product(partials, chosen_group, mask_group)

    outcome = lax.map(
        grouped_both,
        (
            vector_in.reshape(groups, per_group, 2, SECTOR, SECTOR),
            rows_in.reshape(groups, per_group, term_local, ROWS, SECTOR),
            slot_coupling.reshape(groups, per_group, term_local),
            incoming_local.reshape(groups, per_group),
            column_mask.reshape(groups, per_group, SECTOR),
        ),
    )
    outcome = outcome.reshape(slot_count, 2, ROWS, SECTOR)
    returned_rows = lax.all_to_all(outcome, "sec", split_axis=0, concat_axis=0, tiled=True)
    own_rows = jnp.take(returned_rows, send_slot, axis=0).reshape(SEC_DEV, STATES, 2, ROWS, SECTOR)
    summed = lax.psum_scatter(own_rows, "term", scatter_dimension=3, tiled=True)
    return summed.astype(jnp.bfloat16)


def after(value, *earlier):
    return lax.optimization_barrier((value,) + earlier)[0]


def partner_of(partner, device, n):
    return partner[device * SEC_DEV + lax.shift_right_logical(n, 4), n & (STATES - 1)]


def owner_of(sector):
    return lax.shift_right_logical(sector, 1)


ANY = pl.BlockSpec(memory_space=pl.ANY)
VMEM = pl.BlockSpec(memory_space=pltpu.VMEM)
SMEM = pl.BlockSpec(memory_space=pltpu.SMEM)


def exchange(x, axis, step):
    size = lax.axis_size(axis)
    return lax.ppermute(x, axis, [(i, i ^ step) for i in range(size)])


def exchange_both(x, step, term_step):
    devices, terms = lax.axis_size("sec"), lax.axis_size("term")
    if step == 0:
        return exchange(x, "term", term_step)
    pairs = [
        (s * terms + t, (s ^ step) * terms + (t ^ term_step))
        for s in range(devices)
        for t in range(terms)
    ]
    return lax.ppermute(x, ("sec", "term"), pairs)


def piece_order(size):
    order = [0]
    bit = size // 2
    while bit:
        order = order + [j ^ bit for j in order]
        bit //= 2
    return order


def pack_kernel(devices, terms, partner, wave, *refs):
    sends = refs[: devices - 1]
    counts, table, sems = refs[devices - 1 :]
    capacity = SEC_DEV * STATES // devices
    share = capacity // terms
    me, term = lax.axis_index("sec"), lax.axis_index("term")
    for owner in range(devices):
        counts[owner] = 0

    def place(n, carry):
        owner = owner_of(partner_of(partner, me, n))
        rank = counts[owner]
        counts[owner] = rank + 1
        table[owner * capacity + rank] = n
        return carry

    lax.fori_loop(0, SEC_DEV * STATES, place, 0, unroll=True)
    copies = []
    for step in range(1, devices):
        target = me ^ step
        for sub in range(share):
            n = table[target * capacity + term * share + sub]
            copy = pltpu.make_async_copy(
                wave.at[n], sends[step - 1].at[sub], sems.at[(step - 1) * share + sub]
            )
            copy.start()
            copies.append(copy)
    for copy in copies:
        copy.wait()


def pack(wave, partner, devices, terms):
    capacity = SEC_DEV * STATES // devices
    share = capacity // terms
    piece = jax.ShapeDtypeStruct((share, 2, SECTOR, SECTOR), jnp.bfloat16)
    return pl.pallas_call(
        functools.partial(pack_kernel, devices, terms),
        out_shape=[piece] * (devices - 1),
        in_specs=[SMEM, ANY],
        out_specs=[VMEM] * (devices - 1),
        scratch_shapes=[
            pltpu.SMEM((devices,), jnp.int32),
            pltpu.SMEM((SEC_DEV * STATES,), jnp.int32),
            pltpu.SemaphoreType.DMA(((devices - 1) * share,)),
        ],
        cost_estimate=pl.CostEstimate(flops=0, bytes_accessed=4 << 20, transcendentals=0),
        name="pack",
    )(partner, wave)


def compute_kernel(step, devices, terms, partner, order, *refs):
    coefs, refs = refs[:NEAR], refs[NEAR:]
    pieces = refs[: 1 if step == 0 else terms]
    refs = refs[len(pieces) :]
    lefts, refs = refs[:NEAR], refs[NEAR:]
    rights, (keep, give) = refs[:NEAR], refs[NEAR : 2 + NEAR]
    table, partials, cut = refs[2 + NEAR : 5 + NEAR]
    capacity = SEC_DEV * STATES // devices
    share = capacity // terms
    js = piece_order(terms)
    me, term = lax.axis_index("sec"), lax.axis_index("term")
    source = me ^ step
    group = ROWS // terms
    rows = ROWS // NEAR
    local = lefts[0].shape[1]
    depth = local * SECTOR

    def place(n, count):
        table[count] = n
        owner = owner_of(partner_of(partner, source, n))
        return count + jnp.where(owner == me, 1, 0)

    lax.fori_loop(0, SEC_DEV * STATES, place, 0, unroll=True)
    if step == 0:
        wave, (blocks, sems) = pieces[0], refs[5 + NEAR :]
        copies = []
        for slot in range(capacity):
            copy = pltpu.make_async_copy(wave.at[table[slot]], blocks.at[slot], sems.at[slot])
            copy.start()
            copies.append(copy)
        for copy in copies:
            copy.wait()
    first_core = (term & (NEAR - 1)) == 0
    for i in range(NEAR):
        for a in range(SEC_DEV):
            for t in range(local):
                whole = lefts[i][a, t].astype(jnp.float32)
                parts = [whole[r * group : (r + 1) * group] for r in range(terms)]
                tile = jnp.concatenate(
                    [jnp.where(first_core, parts[r], parts[r + 1]) for r in range(0, terms, NEAR)],
                    axis=0,
                )
                cut[i, a, t * rows : (t + 1) * rows, :] = tile.astype(jnp.bfloat16)
    row_index = lax.broadcasted_iota(jnp.int32, (SECTOR, SECTOR), 0)
    col_index = lax.broadcasted_iota(jnp.int32, (SECTOR, SECTOR), 1)

    def slot_of(j, sub):
        return (term ^ js[j]) * share + sub

    def first(j, sub):
        slot = slot_of(j, sub)
        n = table[slot]
        sector, state = lax.shift_right_logical(n, 4), n & (STATES - 1)
        left_order = order[source * SEC_DEV + sector]
        right_order = order[partner_of(partner, source, n)]
        keep_mask = (row_index < left_order) & (col_index < right_order)
        block = blocks.at[slot] if step == 0 else pieces[j].at[sub]
        vectors = [
            jnp.where(keep_mask, block[v].astype(jnp.float32), 0.0).astype(jnp.bfloat16)
            for v in range(2)
        ]
        both = jnp.concatenate(vectors, axis=1)
        place_row = (j * share + sub) * 2 * rows
        for i in range(NEAR):
            product = jnp.dot(cut[i, sector], both, preferred_element_type=jnp.float32)
            for t in range(local):
                scaled = product[t * rows : (t + 1) * rows] * coefs[i][t, state]
                start = (i * local + t) * SECTOR
                for v in range(2):
                    partials[
                        place_row + v * rows : place_row + (v + 1) * rows, start : start + SECTOR
                    ] = scaled[:, v * SECTOR : (v + 1) * SECTOR].astype(jnp.bfloat16)

    for j in range(terms):
        for sub in range(share):
            first(j, sub)

    total = jnp.zeros((capacity * 2 * rows, SEC_DEV * SECTOR), jnp.float32)
    for i in range(NEAR):
        right = [rights[i][p].reshape(depth, SECTOR) for p in range(SEC_DEV)]
        total = total + jnp.dot(
            partials[:, i * depth : (i + 1) * depth],
            jnp.concatenate(right, axis=1),
            preferred_element_type=jnp.float32,
        )
    column = lax.broadcasted_iota(jnp.int32, (2 * rows, SECTOR), 1)
    near_first = term < NEAR
    for j in range(terms):
        for sub in range(share):
            slot = slot_of(j, sub)
            n = table[slot]
            right_id = partner_of(partner, source, n)
            start = (j * share + sub) * 2 * rows
            mine = total[start : start + 2 * rows]
            result = mine[:, :SECTOR]
            for p in range(1, SEC_DEV):
                result = jnp.where(
                    (right_id & (SEC_DEV - 1)) == p, mine[:, p * SECTOR : (p + 1) * SECTOR], result
                )
            result = jnp.where(column < order[right_id], result, 0.0)
            for v in range(2):
                low = result[v * rows : v * rows + group]
                high = result[v * rows + group : (v + 1) * rows]
                keep[slot, v] = jnp.where(near_first, low, high).astype(keep.dtype)
                give[slot, v] = jnp.where(near_first, high, low).astype(give.dtype)


def compute(step, pieces, lefts, rights, coefs, order, partner, devices, terms):
    capacity = SEC_DEV * STATES // devices
    rows = ROWS // NEAR
    local = lefts[0].shape[1]
    scratch = [
        pltpu.SMEM((SEC_DEV * STATES + 1,), jnp.int32),
        pltpu.VMEM((capacity * 2 * rows, NEAR * local * SECTOR), jnp.bfloat16),
        pltpu.VMEM((NEAR, SEC_DEV, local * rows, SECTOR), jnp.bfloat16),
    ]
    if step == 0:
        scratch += [
            pltpu.VMEM((capacity, 2, SECTOR, SECTOR), jnp.bfloat16),
            pltpu.SemaphoreType.DMA((capacity,)),
        ]
    part = jax.ShapeDtypeStruct((capacity, 2, ROWS // terms, SECTOR), RETURNED)
    return pl.pallas_call(
        functools.partial(compute_kernel, step, devices, terms),
        out_shape=[part, part],
        in_specs=[SMEM] * (2 + NEAR)
        + [ANY if step == 0 else VMEM] * len(pieces)
        + [VMEM] * (2 * NEAR),
        out_specs=[VMEM, VMEM],
        scratch_shapes=scratch,
        compiler_params=pltpu.CompilerParams(vmem_limit_bytes=24 << 20),
        cost_estimate=pl.CostEstimate(
            flops=3 << 30, bytes_accessed=4 << 20, transcendentals=0
        ),
        name=f"products_{step}",
    )(partner, order, *coefs, *pieces, *lefts, *rights)


def unpack_kernel(devices, partner, *refs):
    chunks, (out, counts, table) = refs[: 2 * devices], refs[2 * devices :]
    capacity = SEC_DEV * STATES // devices
    me = lax.axis_index("sec")
    for owner in range(devices):
        counts[owner] = 0

    def place(n, carry):
        owner = owner_of(partner_of(partner, me, n))
        rank = counts[owner]
        counts[owner] = rank + 1
        table[owner * capacity + rank] = n
        return carry

    lax.fori_loop(0, SEC_DEV * STATES, place, 0, unroll=True)
    for step in range(devices):
        for rank in range(capacity):
            near = chunks[2 * step][rank].astype(jnp.float32)
            far = chunks[2 * step + 1][rank].astype(jnp.float32)
            out[table[(me ^ step) * capacity + rank]] = (near + far).astype(jnp.bfloat16)


def unpack(chunks, partner, devices):
    return pl.pallas_call(
        functools.partial(unpack_kernel, devices),
        out_shape=jax.ShapeDtypeStruct((SEC_DEV * STATES,) + chunks[0].shape[1:], jnp.bfloat16),
        in_specs=[SMEM] + [VMEM] * (2 * devices),
        out_specs=VMEM,
        scratch_shapes=[
            pltpu.SMEM((devices,), jnp.int32),
            pltpu.SMEM((SEC_DEV * STATES,), jnp.int32),
        ],
        compiler_params=pltpu.CompilerParams(vmem_limit_bytes=8 << 20),
        cost_estimate=pl.CostEstimate(flops=0, bytes_accessed=1 << 20, transcendentals=0),
        name="unpack",
    )(partner, *chunks)


def paired_body(wavefunction, left_window, right_blocks, couplings, sector_order, partner):
    devices, terms = lax.axis_size("sec"), lax.axis_size("term")
    block_count = SEC_DEV * STATES
    wave = wavefunction.reshape(block_count, 2, SECTOR, SECTOR)
    steps = [2, 3, 1]
    coefs = [couplings, exchange(couplings, "term", 1)]
    rights = [right_blocks, exchange(right_blocks, "term", 1)]
    sends = pack(wave, partner, devices, terms)
    arrived = {step: exchange(sends[step - 1], "sec", step) for step in steps}
    every = list(arrived.values())

    def products(step, vectors, lefts):
        return compute(
            step, vectors, lefts, rights, coefs, sector_order, partner, devices, terms
        )

    left_in = {2: exchange(left_window, "sec", 2)}
    left_in[3] = exchange(after(left_in[2], *every), "sec", 1)
    left_in[1] = exchange(after(left_window, *every), "sec", 1)
    keep, give = products(0, [wave], [left_window, exchange(left_window, "term", 1)])
    chunks = {0: (keep, exchange_both(give, 0, NEAR))}
    first, cross_first = keep, chunks[0][1]
    waits = [keep]
    for step in steps:
        x = exchange(after(arrived[step], left_in[2], arrived[2], first, cross_first), "term", NEAR)
        both = jnp.concatenate([arrived[step], x])
        both, left = lax.optimization_barrier((both, left_in[step], waits[0]))[:2]
        lefts = [left, exchange(left, "term", 1)]
        both = jnp.concatenate([both, exchange(both, "term", 1)])
        lefts[0] = after(lefts[0], *waits)
        keep, give = products(step, jnp.split(both, terms), lefts)
        waits = [keep] + [part for value in list(chunks.values())[-1:] for part in value]
        chunks[step] = (exchange(keep, "sec", step), exchange_both(give, step, NEAR))
    chunks = [part for step in range(devices) for part in chunks[step]]
    out = unpack(chunks, partner, devices)
    return out.reshape(SEC_DEV, STATES, 2, ROWS // terms, SECTOR)


def power_of_two(number):
    return number & (number - 1) == 0


def solution(mesh):
    in_specs = (
        P(("grp", "sec"), None, None, None, None),
        P(("grp", "sec"), "term", None, None),
        P(("grp", "sec"), "term", None, None),
        P("term", None),
        P("grp"),
        P("grp", None),
    )
    out_specs = P(("grp", "sec"), None, None, "term", None)
    devices, terms = mesh.shape["sec"], mesh.shape["term"]
    paired = (
        power_of_two(devices)
        and terms == 2 * NEAR
        and devices <= 8
        and SEC_DEV * STATES % (devices * terms) == 0
        and ROWS == 8 * terms
    )
    body = paired_body if paired else general_body
    return jax.shard_map(body, mesh=mesh, in_specs=in_specs, out_specs=out_specs, check_vma=False)
```
